256 devices in a mesh: sub: 64 (over y, z, core), row: 4 (over x).
Axes of the slice: x: 4, y: 4, z: 8, core: 2. Of those that a mesh axis runs over, the one named last changes fastest.
Arguments:
- displacement_gap: float32 [64, 2304, 128], P('sub', 'row'), may hold values from -30 to 30
- flexibility: float32 [64, 2304, 2304], P('sub', 'row'), may hold values from -1 to 2
- dirichlet: float32 [64, 2304, 2304], P('sub', 'row'), may hold values from -1 to 2
- coupling: float32 [64, 2304, 24], P('sub', 'row'), may hold values from -0.3125 to 0.3125
- coarse_matrix: float32 [768, 768], P('row'), may hold values from -1 to 2, as said below
- labels: int32 [64, 2304], P('sub', 'row'), may hold values from 0 to 4, as said below
- partner: int32 [64, 2304], P('sub', 'row'), may hold values from 0 to 2303, as said below
- corners: int32 [64, 24], P('sub'), may hold values from 0 to 767, as said below
Outputs:
- multipliers: float32 [64, 2304, 128], P('sub', 'row')
- residual: float32 [64, 2304, 128], P('sub', 'row')
The draws below stay inside these ranges and needn't reach their ends.
Inputs may be any that keep to these rules, and one draw needn't show every extreme that they name: `labels`: label 0, 1, 2, 3: the dof is shared with the subdomain 1 after, 1 before, 2 after, 2 before (indices modulo 64); 4: unused. In one row block of 576 dofs at most 144 dofs carry one label 0 to 3, reached; a pair of subdomains shares equally many dofs in each row block from both sides; some subdomain has no unused dof. A used dof's partner lies in the same row block of the neighbouring subdomain, whose partner is the dof itself; an unused dof names its own position. `corners`: distinct within a subdomain; every coarse dof is named by exactly two subdomains. `coarse_matrix`: Symmetric.
All inputs are finite; a program needn't handle non-finite values.
Results may differ from the reference program's by a relative error of at most 0.0003.
Values sent between devices are 32-bit elements; how exact they have to be, the bound alone decides.
No kernel may reach another device: no remote copies, remote signals or barrier semaphores. Data moves between devices by JAX's collectives and lax.ppermute only.
A program may use at most 128 MiB of HBM per device.

```python
import math
import jax
import jax.numpy as jnp
from jax import lax

SUBS = 64
ORDER = 2304
BLOCK = 576
CORNER_DOFS = 24
COARSE = 768
LOADS = 128
ITERS = 3


NEIGHBOUR_SHIFTS = (1, -1, 2, -2)


REVERSED = (1, 0, 3, 2)


def interface_maps(key):
    capacity = BLOCK // 4
    blocks = ORDER // BLOCK
    first_key, second_key, third_key = jax.random.split(key, 3)
    face_counts = jax.random.randint(first_key, (SUBS, blocks), capacity // 2, capacity + 1)
    edge_counts = jax.random.randint(second_key, (SUBS, blocks), capacity // 4, capacity + 1)
    face_counts = face_counts.at[0].set(capacity).at[SUBS - 1].set(capacity)
    edge_counts = edge_counts.at[0].set(capacity).at[SUBS - 2].set(capacity)
    counts = jnp.stack([face_counts, jnp.roll(face_counts, 1, axis=0), edge_counts, jnp.roll(edge_counts, 2, axis=0)], axis=-1)
    bounds = jnp.cumsum(counts, axis=-1)
    positions = jnp.arange(BLOCK, dtype=jnp.int32)
    ordered = jnp.sum((positions[None, None, :, None] >= bounds[:, :, None, :]).astype(jnp.int32), axis=-1)
    subkeys = jax.random.split(third_key, SUBS * blocks)
    shuffles = jax.vmap(lambda subkey: jax.random.permutation(subkey, BLOCK))(subkeys).reshape(SUBS, blocks, BLOCK)
    labels = jnp.take_along_axis(ordered, shuffles, axis=-1)
    grouped = jnp.argsort(labels * BLOCK + positions[None, None, :], axis=-1)
    ranking = jnp.argsort(grouped, axis=-1)
    starts = jnp.concatenate([jnp.zeros_like(bounds[..., :1]), bounds[..., :3]], axis=-1)
    own_start = jnp.take_along_axis(starts, jnp.minimum(labels, 3), axis=-1)
    within = ranking - own_start
    partner = jnp.broadcast_to(positions[None, None, :], labels.shape)
    for heading in range(4):
        offset = NEIGHBOUR_SHIFTS[heading]
        far_order = jnp.roll(grouped, -offset, axis=0)
        far_start = jnp.roll(starts, -offset, axis=0)[..., REVERSED[heading]]
        lookup = jnp.clip(far_start[..., None] + within, 0, BLOCK - 1)
        found = jnp.take_along_axis(far_order, lookup, axis=-1)
        partner = jnp.where(labels == heading, found, partner)
    partner = partner + (jnp.arange(blocks, dtype=jnp.int32) * BLOCK)[None, :, None]
    return (labels.reshape(SUBS, ORDER).astype(jnp.int32), partner.reshape(SUBS, ORDER).astype(jnp.int32))


def symmetric(key, count, blend):
    first_key, second_key, third_key = jax.random.split(key, 3)
    spread = 0.4 / math.sqrt(count)
    uniform_part = jax.random.uniform(first_key, (count, count), minval=-1.0, maxval=1.0) * math.sqrt(3.0)
    normal_part = jnp.clip(jax.random.normal(second_key, (count, count)), -5.0, 5.0)
    raw_values = blend * uniform_part + (1.0 - blend) * normal_part
    off_diagonal = (raw_values + raw_values.T) * (spread / math.sqrt(2.0))
    diagonal = jax.random.uniform(third_key, (count,), minval=1.0, maxval=2.0)
    indices = jnp.arange(count)
    return jnp.where(indices[:, None] == indices[None, :], diagonal[None, :], off_diagonal).astype(jnp.float32)


def draw_labels(key, part):
    return interface_maps(key)[0]


def draw_partner(key, part):
    return interface_maps(key)[1]


def draw_corners(key, part):
    key = jax.random.fold_in(key, 7)
    half_count = CORNER_DOFS // 2
    first_key, second_key, third_key = jax.random.split(key, 3)
    own_set = jax.vmap(lambda subkey: jax.random.permutation(subkey, half_count))(jax.random.split(first_key, SUBS))
    next_set = jax.vmap(lambda subkey: jax.random.permutation(subkey, half_count))(jax.random.split(second_key, SUBS))
    first_index = jnp.arange(SUBS, dtype=jnp.int32) * half_count
    first_half = first_index[:, None] + own_set
    second_half = jnp.roll(first_index, -1)[:, None] + next_set
    joined = jnp.concatenate([first_half, second_half], axis=1)
    shuffles = jax.vmap(lambda subkey: jax.random.permutation(subkey, CORNER_DOFS))(jax.random.split(third_key, SUBS))
    return jnp.take_along_axis(joined, shuffles, axis=1).astype(jnp.int32)


def draw_displacement_gap(key, part):
    key = jax.random.fold_in(key, 31)
    first_key, second_key, third_key = jax.random.split(key, 3)
    growth = 3.0 ** (jnp.arange(SUBS, dtype=jnp.float32) / (SUBS - 1))
    growth = growth[:, None, None]
    values = jnp.clip(jax.random.normal(first_key, (SUBS, ORDER, LOADS)), -4.0, 4.0) * growth
    return values.astype(jnp.float32)


def draw_flexibility(key, part):
    key = jax.random.fold_in(key, 13)
    blend = 1.0
    return lax.map(lambda subkey: symmetric(subkey, ORDER, blend), jax.random.split(key, SUBS))


def draw_dirichlet(key, part):
    key = jax.random.fold_in(key, 17)
    blend = 1.0
    return lax.map(lambda subkey: symmetric(subkey, ORDER, blend), jax.random.split(key, SUBS))


def draw_coarse_matrix(key, part):
    key = jax.random.fold_in(key, 19)
    blend = 1.0
    return symmetric(key, COARSE, blend)


def level_of(rng, dims, cuts, low, top_value):
    level = 1.0
    for dim, parts in cuts:
        steps = jax.random.uniform(jax.random.fold_in(jax.random.fold_in(rng, 6), dim), (parts,), jnp.float32, low / len(cuts), top_value / len(cuts))
        level = level * jnp.repeat(jnp.exp(steps), dims[dim] // parts).reshape((-1,) + (1,) * (len(dims) - 1 - dim))
    return level


def normal_values(own_key, extent, deviation, reach, pieces=(), kind=jnp.bfloat16):
    loudness = level_of(own_key, extent, pieces, -0.22, 0.18) if pieces else 1.0
    values = jax.random.normal(own_key, extent, jnp.float32) * deviation * loudness
    return jnp.minimum(jnp.maximum(values, -reach), reach).astype(kind)


def setup_inputs(seed: int = 0) -> dict:
    splits = jax.random.split(jax.random.key(seed), 9)
    displacement_gap = draw_displacement_gap(jax.random.fold_in(splits[8], 71), 0)
    flexibility = draw_flexibility(jax.random.fold_in(splits[8], 71), 0)
    dirichlet = draw_dirichlet(jax.random.fold_in(splits[8], 71), 0)
    coupling = normal_values(splits[3], (SUBS, ORDER, CORNER_DOFS), (ORDER // 6) ** -0.5, 0.3125, ((0, 64), (1, 4)), jnp.float32)
    coarse_matrix = draw_coarse_matrix(jax.random.fold_in(splits[8], 71), 0)
    labels = draw_labels(jax.random.fold_in(splits[8], 71), 0)
    partner = draw_partner(jax.random.fold_in(splits[8], 71), 0)
    corners = draw_corners(jax.random.fold_in(splits[8], 71), 0)
    return {"displacement_gap": displacement_gap, "flexibility": flexibility, "dirichlet": dirichlet, "coupling": coupling, "coarse_matrix": coarse_matrix, "labels": labels, "partner": partner, "corners": corners}


NEIGHBOUR_SHIFTS = (1, -1, 2, -2)
HIGHEST_PRECISION = lax.Precision.HIGHEST

def interface_jump(values, labels, partner):
    partner_value = jnp.zeros_like(values)
    for heading in range(4):
        rolled = jnp.roll(values, -NEIGHBOUR_SHIFTS[heading], axis=0)
        picked = jax.vmap(lambda source, index: source[index])(rolled, partner)
        partner_value = partner_value + jnp.where((labels == heading)[:, :, None], picked, 0.0)
    return jnp.where((labels < 4)[:, :, None], values - partner_value, 0.0)

def apply_dense(matrix, vector):
    return jnp.einsum('smn,snr->smr', matrix, vector, precision=HIGHEST_PRECISION)

def corner_part(coupling, corners, factor, vector):
    local_load = jnp.einsum('smc,smr->scr', coupling, vector, precision=HIGHEST_PRECISION)
    coarse_load = jax.ops.segment_sum(local_load.reshape(-1, LOADS), corners.reshape(-1), num_segments=COARSE)
    solved = jax.scipy.linalg.cho_solve((factor, True), coarse_load)
    return jnp.einsum('smc,scr->smr', coupling, solved[corners], precision=HIGHEST_PRECISION)

def reference(displacement_gap, flexibility, dirichlet, coupling, coarse_matrix, labels, partner, corners):
    factor = jnp.linalg.cholesky(coarse_matrix)

    def apply_flex(vector):
        mapped = apply_dense(flexibility, vector) + corner_part(coupling, corners, factor, vector)
        return interface_jump(mapped, labels, partner)

    def precondition(vector):
        return interface_jump(apply_dense(dirichlet, vector), labels, partner)

    def inner_product(first, second):
        return jnp.sum(first * second, axis=(0, 1))
    residual = interface_jump(displacement_gap, labels, partner)
    multipliers = jnp.zeros_like(residual)
    search_dir = precondition(residual)
    residual_dot = inner_product(residual, search_dir)
    for sweep in range(ITERS):
        mapped = apply_flex(search_dir)
        step_length = residual_dot / inner_product(search_dir, mapped)
        multipliers = multipliers + step_length * search_dir
        residual = residual - step_length * mapped
        if sweep + 1 < ITERS:
            smoothed = precondition(residual)
            next_dot = inner_product(residual, smoothed)
            search_dir = smoothed + next_dot / residual_dot * search_dir
            residual_dot = next_dot
    return (multipliers, residual)
```

```python
import functools

import jax
import jax.numpy as jnp
from jax import lax
from jax.experimental import pallas as pl
from jax.experimental.pallas import tpu as pltpu
from jax.sharding import PartitionSpec as P

ITERS = 3
LANES = 128
PANEL = 128
HIGHEST_PRECISION = lax.Precision.HIGHEST
F32, BF16 = jnp.float32, jnp.bfloat16
VMEM = pl.BlockSpec(memory_space=pltpu.VMEM)
SMEM = pl.BlockSpec(memory_space=pltpu.SMEM)


def call(kernel, outs, *args, scalars=0, scratch=(), flops=10**8, vmem=40, alias=None):
    return pl.pallas_call(
        kernel,
        out_shape=[jax.ShapeDtypeStruct(shape, dtype) for shape, dtype in outs],
        in_specs=[SMEM] * scalars + [VMEM] * (len(args) - scalars),
        out_specs=[VMEM] * len(outs),
        scratch_shapes=list(scratch),
        input_output_aliases=alias or {},
        cost_estimate=pl.CostEstimate(flops=flops, bytes_accessed=10**6, transcendentals=0),
        compiler_params=pltpu.CompilerParams(vmem_limit_bytes=vmem * 2**20),
    )(*args)


def dot(left, right):
    return jnp.dot(left, right, preferred_element_type=F32)


def exact(left, right):
    return jnp.dot(left, right, precision=HIGHEST_PRECISION, preferred_element_type=F32)


def halves(value):
    high = value.astype(BF16)
    return high, (value - high.astype(F32)).astype(BF16)


def thirds(value):
    high = value.astype(BF16)
    rest = value - high.astype(F32)
    middle = rest.astype(BF16)
    return high, middle, (rest - middle.astype(F32)).astype(BF16)


def select_rows(chooser, value):
    cols = value.shape[1]
    found = dot(chooser, jnp.concatenate(thirds(value), axis=1))
    return found[:, :cols] + (found[:, cols : 2 * cols] + found[:, 2 * cols :])


def write_packets(packets, chooser, value):
    packed = select_rows(chooser, value)
    slots = packed.shape[0] // 4
    for k in range(4):
        packets[k][...] = packed[k * slots : (k + 1) * slots]


def apply_rows(high, low, vector, out):
    first, second = halves(vector)
    both = jnp.concatenate([first, second], axis=1)
    tile = high.shape[0] // 4

    def body(i, carry):
        rows = pl.ds(pl.multiple_of(i * tile, 16), tile)
        wide = dot(high[rows, :], both)
        out[rows, :] = wide[:, :LANES] + (wide[:, LANES:] + dot(low[rows, :], first))
        return carry

    lax.fori_loop(0, 4, body, 0)


def assemble(row, blocks, full):
    rows = full.shape[0] // 4
    for k in range(4):
        origin = lax.rem(row[0] - k + 4, 4)
        full[pl.ds(pl.multiple_of(origin * rows, 64), rows), :] = blocks[k][:rows, :]


def own_rows(row, full):
    rows = full.shape[0] // 4
    return full[pl.ds(pl.multiple_of(row[0] * rows, 64), rows), :]


def by_row(row, choices):
    picked = choices[0]
    for k in range(1, 4):
        picked = jnp.where(row[0] == k, choices[k], picked)
    return picked


def col_sum(first, second):
    return jnp.sum(first * second, axis=0, keepdims=True)


def prepare_kernel(role_r, role_c, part_r, part_c, gap, sender, taker, used, p0, p1, p2, p3):
    n = gap.shape[0]
    slots = n // 4
    down = lax.broadcasted_iota(jnp.int32, (n, n), 0)
    across = lax.broadcasted_iota(jnp.int32, (n, n), 1)
    same = role_c[...] == role_r[...]
    rank = jnp.sum(jnp.where(same & (down < across), 1, 0), axis=0, keepdims=True)
    sender[...] = jnp.where(down == role_r[...] * slots + rank, 1.0, 0.0).astype(BF16)
    rank = jnp.sum(jnp.where(same & (part_r[...] < part_c[...]), 1, 0), axis=1, keepdims=True)
    taker[...] = jnp.where(across == role_c[...] * slots + rank, 1.0, 0.0).astype(BF16)
    used[...] = jnp.broadcast_to(jnp.where(role_c[...] < 4, 1.0, 0.0), used.shape)
    write_packets((p0, p1, p2, p3), sender[...], gap[...])


def split_kernel(matrix, high, low):
    high[...], low[...] = halves(matrix[...])


def jump_of(value, arrived, taker, used):
    got = jnp.concatenate([a[...] for a in arrived], axis=0)
    return jnp.where(used[...] > 0, value[...], 0.0) - select_rows(taker[...], got)


def jump_kernel(value, a0, a1, a2, a3, taker, used, out):
    out[...] = jump_of(value, (a0, a1, a2, a3), taker, used)


def jump_load_kernel(value, a0, a1, a2, a3, taker, used, coupling_t, out):
    n = value.shape[0]
    jumped = jump_of(value, (a0, a1, a2, a3), taker, used)
    out[:n, :] = jumped
    out[n:, :] = exact(coupling_t[...], jumped)


def dirichlet_kernel(row, b0, b1, b2, b3, high, low, sender, full, image, p0, p1, p2, p3):
    assemble(row, (b0, b1, b2, b3), full)
    apply_rows(high, low, full[...], image)
    write_packets((p0, p1, p2, p3), sender[...], image[...])


def load_rows(row, blocks):
    n = 576 if False else blocks[0].shape[0] - 24
    load = blocks[0][n:, :] + blocks[1][n:, :] + (blocks[2][n:, :] + blocks[3][n:, :])
    return by_row(row, [load[6 * k : 6 * k + 6] for k in range(4)])


def send_first_kernel(row, b0, b1, b2, b3, corner_rows, full, send):
    assemble(row, (b0, b1, b2, b3), full)
    piece = jnp.concatenate(
        [load_rows(row, (b0, b1, b2, b3)), jnp.zeros((2, LANES), F32), corner_rows[...]], axis=0
    )
    for k in range(send.shape[0] // 16):
        send[16 * k : 16 * k + 16, :] = piece


def send_kernel(row, b0, b1, b2, b3, residual, pre, image, search, full, send):
    assemble(row, (b0, b1, b2, b3), full)
    first = col_sum(residual[...], pre[...])
    second = col_sum(residual[...], full[...]) + col_sum(image[...], pre[...])
    third = col_sum(image[...], full[...])
    fourth = col_sum(search[...], image[...])
    piece = jnp.concatenate(
        [
            load_rows(row, (b0, b1, b2, b3)),
            by_row(row, [first, second, third, fourth]),
            jnp.zeros((1, LANES), F32),
        ],
        axis=0,
    )
    for k in range(send.shape[0] // 8):
        send[8 * k : 8 * k + 8, :] = piece


def solve_first_kernel(got, inverse, corner_col, mixer, out):
    subs = got.shape[0] // 16
    coarse = inverse.shape[0]
    split = got[...].reshape(subs, 16, LANES)
    loads = split[:, :8].reshape(subs * 8, LANES)
    names = split[:, 8:].reshape(subs * 8, LANES).astype(jnp.int32)
    lane = lax.broadcasted_iota(jnp.int32, (subs * 8, LANES), 1)
    slot = lax.broadcasted_iota(jnp.int32, (subs * 8, LANES), 0)
    real = lax.rem(slot, 8) < 6
    spread = jnp.concatenate(
        [
            jnp.where(real & (names == lane + k * LANES), 1.0, 0.0).astype(BF16)
            for k in range(coarse // LANES)
        ],
        axis=1,
    )
    wide = lax.broadcasted_iota(jnp.int32, (corner_col.shape[0], coarse), 1)
    own = jnp.where(corner_col[...] == wide, 1.0, 0.0).astype(BF16)
    chosen = select_rows(own, inverse[...])
    total = None
    for part in thirds(chosen):
        term = lax.dot_general(
            part, spread, (((1,), (1,)), ((), ())), preferred_element_type=F32
        )
        total = term if total is None else total + term
    mixer[...] = total
    out[:24, :] = exact(total, loads)
    out[24:, :] = jnp.zeros((8, LANES), F32)


def solve_kernel(row, got, mixer, out):
    subs = got.shape[0] // 8
    out[:24, :] = exact(mixer[...], got[...])
    value = jnp.sum(got[...].reshape(subs, 8, LANES), axis=0)[6:7]
    place = lax.broadcasted_iota(jnp.int32, (8, LANES), 0)
    out[24:, :] = jnp.where(place == row[0], jnp.broadcast_to(value, (8, LANES)), 0.0)


def flex_first_kernel(s0, s1, s2, s3, search, high, low, coupling, sender, solved, out, p0, p1, p2, p3):
    total = (s0[...] + s1[...]) + (s2[...] + s3[...])
    solved[...] = total[:24]
    apply_rows(high, low, search[...], out)
    out[...] = out[...] + exact(coupling[...], solved[...])
    write_packets((p0, p1, p2, p3), sender[...], out[...])


def flex_kernel(
    last, row, s0, s1, s2, s3, residual, pre, step, image, search, solved_pre, solved, sums,
    high, low, coupling, sender,
    new_residual, new_pre, new_search, new_solved_pre, new_solved, new_sums, out, p0, p1, p2, p3,
    *send,
):
    total = (s0[...] + s1[...]) + (s2[...] + s3[...])
    rho, cross, square, energy = total[24:25], total[25:26], total[26:27], total[27:28]
    alpha = rho / energy
    next_rho = rho - alpha * cross + alpha * alpha * square
    beta = next_rho / rho
    new_sums[...] = sums[...] + alpha * own_rows(row, search)
    new_residual[...] = residual[...] - alpha * image[...]
    new_pre[...] = pre[...] - alpha * step[...]
    new_search[...] = new_pre[...] + beta * search[...]
    new_solved_pre[...] = solved_pre[...] - alpha * total[:24]
    new_solved[...] = new_solved_pre[...] + beta * solved[...]
    apply_rows(high, low, new_search[...], out)
    out[...] = out[...] + exact(coupling[...], new_solved[...])
    write_packets((p0, p1, p2, p3), sender[...], out[...])
    if last:
        pair = jnp.concatenate(
            [
                col_sum(own_rows(row, new_residual), own_rows(row, new_pre)),
                2.0 * col_sum(own_rows(row, new_search), out[...]),
            ]
            * 4,
            axis=0,
        )
        for k in range(send[0].shape[0] // 8):
            send[0][8 * k : 8 * k + 8, :] = pair


def finish_kernel(row, got, value, a0, a1, a2, a3, taker, used, residual, search, sums, out_sums, out_residual):
    total = jnp.sum(got[...].reshape(got.shape[0] // 8, 8, LANES), axis=0)
    total = (total[0:2] + total[2:4]) + (total[4:6] + total[6:8])
    alpha = total[0:1] / total[1:2]
    image = jump_of(value, (a0, a1, a2, a3), taker, used)
    out_sums[...] = sums[...] + alpha * own_rows(row, search)
    out_residual[...] = own_rows(row, residual) - alpha * image


def invert_panel(matrix):
    size = matrix.shape[0]
    down = lax.broadcasted_iota(jnp.int32, (size, size), 0)
    across = lax.broadcasted_iota(jnp.int32, (size, size), 1)
    for k in range(size):
        column = jnp.broadcast_to(matrix[:, k : k + 1], (size, size))
        scaled = jnp.where(across[:1] == k, 1.0, matrix[k : k + 1, :]) / column[k : k + 1, :]
        cleared = jnp.where(across == k, 0.0, matrix) - column * scaled
        matrix = jnp.where(down == k, jnp.broadcast_to(scaled, (size, size)), cleared)
    return matrix


def eliminate(number, source, out):
    size = source.shape[0]
    panel = slice(number * PANEL, (number + 1) * PANEL)
    column = source[:, panel]
    inverse = invert_panel(source[panel, panel])
    scaled = exact(inverse, source[panel, :])
    here = lax.broadcasted_iota(jnp.int32, (PANEL, size), 1) // PANEL == number
    scaled = jnp.where(here, jnp.concatenate([inverse] * (size // PANEL), axis=1), scaled)
    for i in range(size // PANEL):
        rows = slice(i * PANEL, (i + 1) * PANEL)
        if i == number:
            out[rows, :] = scaled
        else:
            out[rows, :] = jnp.where(here, 0.0, source[rows, :]) - exact(column[rows, :], scaled)


def invert_first_kernel(row, b0, b1, b2, b3, out, whole):
    assemble(row, (b0, b1, b2, b3), whole)
    eliminate(0, whole, out)


def invert_kernel(number, source, out):
    eliminate(number, source, out)


def row_blocks(value):
    count = lax.axis_size("row")
    moved = [value]
    for k in range(1, 4):
        moved.append(lax.ppermute(value, "row", [(i, (i + k) % count) for i in range(count)]))
    return moved


def exchange(packets):
    count = lax.axis_size("sub")
    mate = [(i, i ^ 1) for i in range(count)]
    other = [(i, (i + (1 if i % 2 else -1)) % count) for i in range(count)]
    ahead = [(i, (i + 2) % count) for i in range(count)]
    behind = [(i, (i - 2) % count) for i in range(count)]
    return (
        lax.ppermute(packets[0], "sub", mate),
        lax.ppermute(packets[1], "sub", other),
        lax.ppermute(packets[3], "sub", behind),
        lax.ppermute(packets[2], "sub", ahead),
    )


def local(displacement_gap, flexibility, dirichlet, coupling, coarse_matrix, labels, partner, corners):
    gap = displacement_gap[0]
    n = gap.shape[0]
    order = flexibility.shape[2]
    subs = lax.axis_size("sub")
    coarse = coarse_matrix.shape[1]
    row_index = lax.axis_index("row").astype(jnp.int32)
    row = row_index.reshape(1)
    block, full, packet = ((n, LANES), F32), ((order, LANES), F32), ((n // 4, LANES), F32)
    square = ((n, n), BF16)

    coarse_blocks = row_blocks(coarse_matrix)

    parity = lax.axis_index("sub").astype(jnp.int32) % 2
    own_labels = labels[0]
    role = jnp.where(own_labels < 2, own_labels ^ parity, own_labels)
    sender, taker, used, *packets = call(
        prepare_kernel, [square, square, block] + [packet] * 4,
        role[None, :], role[:, None], partner[0][None, :], partner[0][:, None], gap, flops=10**9,
    )

    def split(matrix):
        rows = n // 4
        spec = pl.BlockSpec((rows, order), lambda i: (i, 0))
        return pl.pallas_call(
            split_kernel,
            grid=(4,),
            out_shape=[jax.ShapeDtypeStruct((n, order), BF16)] * 2,
            in_specs=[spec],
            out_specs=[spec] * 2,
            cost_estimate=pl.CostEstimate(flops=10**8, bytes_accessed=4 * 2 * n * order, transcendentals=0),
            compiler_params=pltpu.CompilerParams(vmem_limit_bytes=40 * 2**20),
        )(matrix)

    dirichlet_parts = split(dirichlet[0])
    flex_parts = split(flexibility[0])
    couple = coupling[0]
    couple_t = couple.T

    def jump(value, packets):
        return call(jump_kernel, [block], value, *exchange(packets), taker, used)[0]

    def jump_load(value, packets):
        return call(
            jump_load_kernel, [((n + 24, LANES), F32)], value, *exchange(packets), taker, used, couple_t
        )[0]

    def apply_dirichlet(own):
        whole, image, *packets = call(
            dirichlet_kernel, [full, block] + [packet] * 4,
            row, *row_blocks(own), *dirichlet_parts, sender, scalars=1, flops=10**9,
        )
        return whole, image, packets

    residual, image, packets = apply_dirichlet(jump(gap, packets))

    [inverse] = call(
        invert_first_kernel, [((coarse, coarse), F32)], row, *coarse_blocks,
        scalars=1, flops=8 * 10**9, scratch=[pltpu.VMEM((coarse, coarse), F32)],
    )
    for number in range(1, coarse // PANEL):
        [inverse] = call(
            functools.partial(invert_kernel, number), [((coarse, coarse), F32)], inverse, flops=8 * 10**9
        )

    own_corners = corners[0]
    mine = lax.dynamic_slice(own_corners, (6 * row_index,), (6,)).astype(F32)
    corner_rows = jnp.broadcast_to(jnp.concatenate([mine, mine[:2]])[:, None], (8, LANES))

    pre, send = call(
        send_first_kernel, [full, ((16 * subs, LANES), F32)],
        row, *row_blocks(jump_load(image, packets)), corner_rows, scalars=1,
    )
    got = lax.all_to_all(send, "sub", 0, 0, tiled=True)
    mixer, solved = call(
        solve_first_kernel, [((24, 8 * subs), F32), ((32, LANES), F32)], got, inverse, own_corners[:, None]
    )

    search = pre
    solved_pre, value, *packets = call(
        flex_first_kernel, [((24, LANES), F32), block] + [packet] * 4,
        *row_blocks(solved), search, *flex_parts, couple, sender, flops=10**9,
    )
    solved_search = solved_pre
    sums = jnp.zeros((n, LANES), F32)
    for sweep in range(1, ITERS):
        last = sweep == ITERS - 1
        image, value, packets = apply_dirichlet(jump(value, packets))
        step, send = call(
            send_kernel, [full, ((8 * subs, LANES), F32)],
            row, *row_blocks(jump_load(value, packets)), residual, pre, image, search, scalars=1,
        )
        got = lax.all_to_all(send, "sub", 0, 0, tiled=True)
        [solved] = call(solve_kernel, [((32, LANES), F32)], row, got, mixer, scalars=1)
        outs = [full] * 3 + [((24, LANES), F32)] * 2 + [block] * 2 + [packet] * 4
        if last:
            outs = outs + [((2 * subs * 4, LANES), F32)]
        residual, pre, search, solved_pre, solved_search, sums, value, *packets = call(
            functools.partial(flex_kernel, last), outs,
            row, *row_blocks(solved), residual, pre, step, image, search, solved_pre, solved_search, sums,
            *flex_parts, couple, sender, scalars=1, flops=10**9,
        )
    *packets, send = packets
    got = lax.all_to_all(send, ("sub", "row"), 0, 0, tiled=True)
    sums, out = call(
        finish_kernel, [block, block], row, got, value, *exchange(packets), taker, used,
        residual, search, sums, scalars=1,
    )
    return (sums[None], out[None])


def solution(mesh):
    in_specs = (
        P("sub", "row", None),
        P("sub", "row", None),
        P("sub", "row", None),
        P("sub", "row", None),
        P("row", None),
        P("sub", "row"),
        P("sub", "row"),
        P("sub", None),
    )
    out_specs = (P("sub", "row", None), P("sub", "row", None))
    return jax.shard_map(local, mesh=mesh, in_specs=in_specs, out_specs=out_specs, check_vma=False)
```

```python
import functools

import jax
import jax.numpy as jnp
from jax import lax
from jax.experimental import pallas as pl
from jax.experimental.pallas import tpu as pltpu
from jax.sharding import PartitionSpec as P

ITERS = 3
LANES = 128
PANEL = 128
GROUP = 4
HIGHEST_PRECISION = lax.Precision.HIGHEST
F32, BF16 = jnp.float32, jnp.bfloat16
VMEM = pl.BlockSpec(memory_space=pltpu.VMEM)
SMEM = pl.BlockSpec(memory_space=pltpu.SMEM)
ANY = pl.BlockSpec(memory_space=pl.ANY)


def call(kernel, outs, *args, scalars=0, scratch=(), flops=10**8, vmem=12, loose=0):
    return pl.pallas_call(
        kernel,
        out_shape=[jax.ShapeDtypeStruct(shape, dtype) for shape, dtype in outs],
        in_specs=[SMEM] * scalars + [VMEM] * (len(args) - scalars - loose) + [ANY] * loose,
        out_specs=[VMEM] * len(outs),
        scratch_shapes=list(scratch),
        cost_estimate=pl.CostEstimate(flops=flops, bytes_accessed=10**6, transcendentals=0),
        compiler_params=pltpu.CompilerParams(vmem_limit_bytes=vmem * 2**20),
    )(*args)


def dot(left, right):
    return jnp.dot(left, right, preferred_element_type=F32)


def exact(left, right):
    return jnp.dot(left, right, precision=HIGHEST_PRECISION, preferred_element_type=F32)


def halves(value):
    high = value.astype(BF16)
    return high, (value - high.astype(F32)).astype(BF16)


def thirds(value):
    high = value.astype(BF16)
    rest = value - high.astype(F32)
    middle = rest.astype(BF16)
    return high, middle, (rest - middle.astype(F32)).astype(BF16)


def select_rows(chooser, value):
    cols = value.shape[1]
    found = dot(chooser, jnp.concatenate(thirds(value), axis=1))
    return found[:, :cols] + (found[:, cols : 2 * cols] + found[:, 2 * cols :])


def write_packets(packets, chooser, value):
    packed = select_rows(chooser, value)
    slots = packed.shape[0] // 4
    for k in range(4):
        packets[k][...] = packed[k * slots : (k + 1) * slots]


def apply_rows(high, low, vector, out):
    first, second = halves(vector)
    both = jnp.concatenate([first, second], axis=1)
    tile = high.shape[0] // 4

    def body(i, carry):
        rows = pl.ds(pl.multiple_of(i * tile, 16), tile)
        wide = dot(high[rows, :], both)
        out[rows, :] = wide[:, :LANES] + (wide[:, LANES:] + dot(low[rows, :], first))
        return carry

    lax.fori_loop(0, 4, body, 0)


def assemble(row, blocks, full):
    rows = full.shape[0] // 4
    for k in range(4):
        origin = lax.rem(row[0] - k + 4, 4)
        full[pl.ds(pl.multiple_of(origin * rows, 64), rows), :] = blocks[k][:rows, :]


def own_rows(row, full):
    rows = full.shape[0] // 4
    return full[pl.ds(pl.multiple_of(row[0] * rows, 64), rows), :]


def by_row(row, choices):
    picked = choices[0]
    for k in range(1, 4):
        picked = jnp.where(row[0] == k, choices[k], picked)
    return picked


def col_sum(first, second):
    return jnp.sum(first * second, axis=0, keepdims=True)


def prepare_kernel(parity, labels, partner, gap, sender, taker, used, p0, p1, p2, p3):
    n = gap.shape[0]
    slots = n // 4
    down = lax.broadcasted_iota(jnp.int32, (n, n), 0)
    across = lax.broadcasted_iota(jnp.int32, (n, n), 1)
    label, part_r = labels[...], partner[...]
    flipped = jnp.where(label == 0, parity[0], 1 - parity[0])
    role_r = jnp.where(label < 2, flipped, label)
    diagonal = down == across
    role_c = jnp.sum(jnp.where(diagonal, role_r, 0), axis=1, keepdims=True)
    part_c = jnp.sum(jnp.where(diagonal, part_r, 0), axis=1, keepdims=True)
    same = role_c == role_r
    rank = jnp.sum(jnp.where(same & (down < across), 1, 0), axis=0, keepdims=True)
    sender[...] = jnp.where(down == role_r * slots + rank, 1.0, 0.0).astype(BF16)
    rank = jnp.sum(jnp.where(same & (part_r < part_c), 1, 0), axis=1, keepdims=True)
    taker[...] = jnp.where(across == role_c * slots + rank, 1.0, 0.0).astype(BF16)
    used[...] = jnp.broadcast_to(jnp.where(role_c < 4, 1.0, 0.0), used.shape)
    write_packets((p0, p1, p2, p3), sender[...], gap[...])


def split_kernel(matrix, high, low):
    high[...], low[...] = halves(matrix[...])


def jump_of(value, arrived, taker, used):
    got = jnp.concatenate([a[...] for a in arrived], axis=0)
    return jnp.where(used[...] > 0, value[...], 0.0) - select_rows(taker[...], got)


def jump_kernel(value, a0, a1, a2, a3, taker, used, *rest):
    rest[-1][...] = jump_of(value, (a0, a1, a2, a3), taker, used)


def write_pieces(out, load, scalars):
    for k in range(4):
        out[8 * k : 8 * k + 8, :] = jnp.concatenate(
            [load[6 * k : 6 * k + 6], scalars[k], jnp.zeros((1, LANES), F32)], axis=0
        )


def jump_first_load_kernel(value, a0, a1, a2, a3, taker, used, coupling_t, out, pieces):
    jumped = jump_of(value, (a0, a1, a2, a3), taker, used)
    out[...] = jumped
    write_pieces(pieces, exact(coupling_t[...], jumped), [jnp.zeros((1, LANES), F32)] * 4)


def jump_load_kernel(
    row, value, a0, a1, a2, a3, taker, used, coupling_t, residual, pre, image, search, out, pieces
):
    jumped = jump_of(value, (a0, a1, a2, a3), taker, used)
    out[...] = jumped
    own_residual, own_pre = own_rows(row, residual), own_rows(row, pre)
    own_image, own_search = own_rows(row, image), own_rows(row, search)
    scalars = [
        col_sum(own_residual, own_pre),
        col_sum(own_residual, jumped) + col_sum(own_image, own_pre),
        col_sum(own_image, jumped),
        col_sum(own_search, own_image),
    ]
    write_pieces(pieces, exact(coupling_t[...], jumped), scalars)


def dirichlet_kernel(row, b0, b1, b2, b3, high, low, sender, full, image, p0, p1, p2, p3):
    assemble(row, (b0, b1, b2, b3), full)
    apply_rows(high, low, full[...], image)
    write_packets((p0, p1, p2, p3), sender[...], image[...])


def summed_piece(got):
    return (got[0:8, :] + got[8:16, :]) + (got[16:24, :] + got[24:32, :])


def spread_first_kernel(got, corner_rows, send):
    piece = jnp.concatenate([summed_piece(got), corner_rows[...]], axis=0)
    for k in range(send.shape[0] // 16):
        send[16 * k : 16 * k + 16, :] = piece


def spread_kernel(got, send):
    piece = summed_piece(got)
    for k in range(send.shape[0] // 8):
        send[8 * k : 8 * k + 8, :] = piece


def solve_first_kernel(got, inverse, corner_col, mixer, out):
    subs = got.shape[0] // 16
    coarse = inverse.shape[0]
    split = got[...].reshape(subs, 16, LANES)
    loads = split[:, :8].reshape(subs * 8, LANES)
    names = split[:, 8:].reshape(subs * 8, LANES).astype(jnp.int32)
    lane = lax.broadcasted_iota(jnp.int32, (subs * 8, LANES), 1)
    slot = lax.broadcasted_iota(jnp.int32, (subs * 8, LANES), 0)
    real = lax.rem(slot, 8) < 6
    spread = jnp.concatenate(
        [
            jnp.where(real & (names == lane + k * LANES), 1.0, 0.0).astype(BF16)
            for k in range(coarse // LANES)
        ],
        axis=1,
    )
    wide = lax.broadcasted_iota(jnp.int32, (corner_col.shape[0], coarse), 1)
    own = jnp.where(corner_col[...] == wide, 1.0, 0.0).astype(BF16)
    chosen = select_rows(own, inverse[...])
    total = None
    for part in thirds(chosen):
        term = lax.dot_general(
            part, spread, (((1,), (1,)), ((), ())), preferred_element_type=F32
        )
        total = term if total is None else total + term
    mixer[...] = total
    out[:24, :] = exact(total, loads)
    out[24:, :] = jnp.zeros((8, LANES), F32)


def solve_kernel(row, got, mixer, out):
    subs = got.shape[0] // 8
    out[:24, :] = exact(mixer[...], got[...])
    value = jnp.sum(got[...].reshape(subs, 8, LANES), axis=0)[6:7]
    place = lax.broadcasted_iota(jnp.int32, (8, LANES), 0)
    out[24:, :] = jnp.where(place == row[0], jnp.broadcast_to(value, (8, LANES)), 0.0)


def flex_kernel(row, b0, b1, b2, b3, high, low, full, out):
    assemble(row, (b0, b1, b2, b3), full)
    apply_rows(high, low, full[...], out)


def join_first_kernel(s0, s1, s2, s3, flexed, coupling, sender, solved, out, p0, p1, p2, p3):
    total = (s0[...] + s1[...]) + (s2[...] + s3[...])
    solved[...] = total[:24]
    out[...] = flexed[...] + exact(coupling[...], solved[...])
    write_packets((p0, p1, p2, p3), sender[...], out[...])


def step_lengths(total):
    rho, cross, square, energy = total[24:25], total[25:26], total[26:27], total[27:28]
    alpha = rho / energy
    next_rho = rho - alpha * cross + alpha * alpha * square
    return alpha, next_rho / rho


def join(s0, s1, s2, s3, flex_pre, flex_search, flex_step, solved_pre, solved, coupling, out):
    total = (s0[...] + s1[...]) + (s2[...] + s3[...])
    alpha, beta = step_lengths(total)
    next_flex_pre = flex_pre[...] - alpha * flex_step[...]
    next_flex = next_flex_pre + beta * flex_search[...]
    next_solved_pre = solved_pre[...] - alpha * total[:24]
    next_solved = next_solved_pre + beta * solved[...]
    out[...] = next_flex + exact(coupling[...], next_solved)
    return alpha, beta, next_flex_pre, next_flex, next_solved_pre, next_solved


def join_kernel(
    s0, s1, s2, s3, flex_pre, flex_search, flex_step, solved_pre, solved, coupling, sender,
    lengths, new_flex_pre, new_flex_search, new_solved_pre, new_solved, out, p0, p1, p2, p3,
):
    alpha, beta, *new = join(s0, s1, s2, s3, flex_pre, flex_search, flex_step, solved_pre, solved, coupling, out)
    write_packets((p0, p1, p2, p3), sender[...], out[...])
    new_flex_pre[...], new_flex_search[...], new_solved_pre[...], new_solved[...] = new
    lengths[...] = jnp.concatenate([alpha] * 4 + [beta] * 4, axis=0)


def update_kernel(row, lengths, step, residual, pre, image, search, new_residual, new_pre, new_search, sums):
    alpha, beta = lengths[0:1, :], lengths[4:5, :]
    sums[...] = alpha * own_rows(row, search)
    new_residual[...] = residual[...] - alpha * image[...]
    new_pre[...] = pre[...] - alpha * step[...]
    new_search[...] = new_pre[...] + beta * search[...]


def join_last_kernel(
    row, s0, s1, s2, s3, flex_pre, flex_search, flex_step, solved_pre, solved, coupling, sender,
    step, residual, pre, image, search, sums,
    new_residual, new_search, new_sums, out, p0, p1, p2, p3, send,
):
    alpha, beta, *_ = join(s0, s1, s2, s3, flex_pre, flex_search, flex_step, solved_pre, solved, coupling, out)
    write_packets((p0, p1, p2, p3), sender[...], out[...])
    own_search = own_rows(row, search)
    new_sums[...] = sums[...] + alpha * own_search
    own_pre = own_rows(row, pre) - alpha * step[...]
    new_residual[...] = own_rows(row, residual) - alpha * own_rows(row, image)
    new_search[...] = own_pre + beta * own_search
    pair = jnp.concatenate(
        [col_sum(new_residual[...], own_pre), 2.0 * col_sum(new_search[...], out[...])] * 4, axis=0
    )
    for k in range(send.shape[0] // 8):
        send[8 * k : 8 * k + 8, :] = pair


def finish_kernel(got, value, a0, a1, a2, a3, taker, used, residual, search, sums, out_sums, out_residual):
    total = jnp.sum(got[...].reshape(got.shape[0] // 8, 8, LANES), axis=0)
    total = (total[0:2] + total[2:4]) + (total[4:6] + total[6:8])
    alpha = total[0:1] / total[1:2]
    image = jump_of(value, (a0, a1, a2, a3), taker, used)
    out_sums[...] = sums[...] + alpha * search[...]
    out_residual[...] = residual[...] - alpha * image


def invert_panel(matrix):
    size = matrix.shape[0]
    across = lax.broadcasted_iota(jnp.int32, (size, size), 1)
    lane, across8 = across[:1], across[:8]
    down8 = lax.broadcasted_iota(jnp.int32, (8, size), 0)
    for start in range(0, size, GROUP):
        base = start // 8 * 8
        columns = [
            jnp.broadcast_to(matrix[:, start + j : start + j + 1], (size, size)) for j in range(GROUP)
        ]
        pivots = matrix[base : base + 8, :]
        rest = jnp.where((across >= start) & (across < start + GROUP), 0.0, matrix)
        for j in range(GROUP):
            k = start + j
            column = columns[j]
            inverse = 1.0 / column[k : k + 1, :]
            scaled = jnp.where(lane == k, 1.0, pivots[k - base : k - base + 1, :]) * inverse
            cleared = jnp.where(across8 == k, 0.0, pivots) - column[base : base + 8, :] * scaled
            pivots = jnp.where(down8 == k - base, scaled, cleared)
            rest = rest - column * jnp.where((lane > k) & (lane < start + GROUP), 0.0, scaled)
            for m in range(j + 1, GROUP):
                factor = columns[m][k : k + 1, :] * inverse
                updated = columns[m] - column * factor
                parts = [updated[:base]] if base else []
                parts.append(jnp.where(down8 == k - base, factor, updated[base : base + 8]))
                if base + 8 < size:
                    parts.append(updated[base + 8 :])
                columns[m] = jnp.concatenate(parts, axis=0)
        parts = [rest[:base]] if base else []
        parts.append(pivots)
        if base + 8 < size:
            parts.append(rest[base + 8 :])
        matrix = jnp.concatenate(parts, axis=0)
    return matrix


def eliminate(number, source, out):
    size = source.shape[0]
    panel = slice(number * PANEL, (number + 1) * PANEL)
    column = source[:, panel]
    inverse = invert_panel(source[panel, panel])
    scaled = exact(inverse, source[panel, :])
    here = lax.broadcasted_iota(jnp.int32, (PANEL, size), 1) // PANEL == number
    scaled = jnp.where(here, jnp.concatenate([inverse] * (size // PANEL), axis=1), scaled)
    for i in range(size // PANEL):
        rows = slice(i * PANEL, (i + 1) * PANEL)
        if i == number:
            out[rows, :] = scaled
        else:
            out[rows, :] = jnp.where(here, 0.0, source[rows, :]) - exact(column[rows, :], scaled)


def invert_first_kernel(row, b0, b1, b2, b3, out, whole):
    assemble(row, (b0, b1, b2, b3), whole)
    eliminate(0, whole, out)


def invert_kernel(number, source, out):
    eliminate(number, source, out)


def row_blocks(value):
    count = lax.axis_size("row")
    moved = [value]
    for k in range(1, 4):
        moved.append(lax.ppermute(value, "row", [(i, (i + k) % count) for i in range(count)]))
    return moved


def exchange(packets):
    count = lax.axis_size("sub")
    mate = [(i, i ^ 1) for i in range(count)]
    other = [(i, (i + (1 if i % 2 else -1)) % count) for i in range(count)]
    ahead = [(i, (i + 2) % count) for i in range(count)]
    behind = [(i, (i - 2) % count) for i in range(count)]
    return (
        lax.ppermute(packets[0], "sub", mate),
        lax.ppermute(packets[1], "sub", other),
        lax.ppermute(packets[3], "sub", behind),
        lax.ppermute(packets[2], "sub", ahead),
    )


def local(displacement_gap, flexibility, dirichlet, coupling, coarse_matrix, labels, partner, corners):
    gap = displacement_gap[0]
    n = gap.shape[0]
    order = flexibility.shape[2]
    subs = lax.axis_size("sub")
    coarse = coarse_matrix.shape[1]
    row_index = lax.axis_index("row").astype(jnp.int32)
    row = row_index.reshape(1)
    block, full, packet = ((n, LANES), F32), ((order, LANES), F32), ((n // 4, LANES), F32)
    square = ((n, n), BF16)

    coarse_blocks = row_blocks(coarse_matrix)

    parity = lax.axis_index("sub").astype(jnp.int32) % 2
    sender, taker, used, *packets = call(
        prepare_kernel, [square, square, block] + [packet] * 4,
        parity.reshape(1), labels, partner, gap, scalars=1, flops=10**9, vmem=20,
    )

    def split(matrix):
        rows = n // 4
        spec = pl.BlockSpec((rows, order), lambda i: (i, 0))
        return pl.pallas_call(
            split_kernel,
            grid=(4,),
            out_shape=[jax.ShapeDtypeStruct((n, order), BF16)] * 2,
            in_specs=[spec],
            out_specs=[spec] * 2,
            cost_estimate=pl.CostEstimate(flops=10**8, bytes_accessed=4 * 2 * n * order, transcendentals=0),
            compiler_params=pltpu.CompilerParams(vmem_limit_bytes=12 * 2**20),
        )(matrix)

    dirichlet_parts = split(dirichlet[0])
    flex_parts = split(flexibility[0])
    couple = coupling[0]
    couple_t = couple.T

    def jump(value, packets, *after):
        return call(
            jump_kernel, [block], value, *exchange(packets), taker, used, *after, loose=len(after)
        )[0]

    pieces = ((32, LANES), F32)

    def apply_dirichlet(own):
        whole, image, *packets = call(
            dirichlet_kernel, [full, block] + [packet] * 4,
            row, *row_blocks(own), *dirichlet_parts, sender, scalars=1, flops=2 * 10**9, vmem=20,
        )
        return whole, image, packets

    residual, image, packets = apply_dirichlet(jump(gap, packets, *coarse_blocks))

    [inverse] = call(
        invert_first_kernel, [((coarse, coarse), F32)], row, *coarse_blocks,
        scalars=1, flops=6 * 10**9, vmem=18, scratch=[pltpu.VMEM((coarse, coarse), F32)],
    )
    for number in range(1, coarse // PANEL):
        [inverse] = call(
            functools.partial(invert_kernel, number), [((coarse, coarse), F32)], inverse, flops=6 * 10**9, vmem=18,
        )

    own_corners = corners[0]
    mine = lax.dynamic_slice(own_corners, (6 * row_index,), (6,)).astype(F32)
    corner_rows = jnp.broadcast_to(jnp.concatenate([mine, mine[:2]])[:, None], (8, LANES))

    own_pre, parts = call(
        jump_first_load_kernel, [block, pieces], image, *exchange(packets), taker, used, couple_t
    )
    [send] = call(
        spread_first_kernel, [((16 * subs, LANES), F32)], lax.all_to_all(parts, "row", 0, 0, tiled=True), corner_rows
    )
    got = lax.all_to_all(send, "sub", 0, 0, tiled=True)
    mixer, solved = call(
        solve_first_kernel, [((24, 8 * subs), F32), pieces], got, inverse, own_corners[:, None], vmem=16
    )
    small = ((24, LANES), F32)

    def apply_flex(own):
        return call(
            flex_kernel, [full, block], row, *row_blocks(own), *flex_parts, scalars=1, flops=2 * 10**9, vmem=20
        )

    pre, flex_pre = apply_flex(own_pre)
    solved_pre, value, *packets = call(
        join_first_kernel, [small, block] + [packet] * 4, *row_blocks(solved), flex_pre, couple, sender
    )
    search, flex_search, solved_search = pre, flex_pre, solved_pre
    for sweep in range(1, ITERS):
        image, value, packets = apply_dirichlet(jump(value, packets))
        own_step, parts = call(
            jump_load_kernel, [block, pieces],
            row, value, *exchange(packets), taker, used, couple_t, residual, pre, image, search, scalars=1, vmem=16,
        )
        [send] = call(
            spread_kernel, [((8 * subs, LANES), F32)], lax.all_to_all(parts, "row", 0, 0, tiled=True)
        )
        got = lax.all_to_all(send, "sub", 0, 0, tiled=True)
        step, flex_step = apply_flex(own_step)
        [solved] = call(solve_kernel, [((32, LANES), F32)], row, got, mixer, scalars=1)
        joined = (*row_blocks(solved), flex_pre, flex_search, flex_step, solved_pre, solved_search, couple, sender)
        if sweep < ITERS - 1:
            lengths, flex_pre, flex_search, solved_pre, solved_search, value, *packets = call(
                join_kernel, [((8, LANES), F32)] + [block] * 2 + [small] * 2 + [block] + [packet] * 4, *joined
            )
            residual, pre, search, sums = call(
                update_kernel, [full] * 3 + [block], row, lengths, step, residual, pre, image, search,
                scalars=1, vmem=16,
            )
        else:
            residual, search, sums, value, *packets, send = call(
                join_last_kernel, [block] * 4 + [packet] * 4 + [((8 * subs, LANES), F32)],
                row, *joined, own_step, residual, pre, image, search, sums, scalars=1, vmem=16,
            )
    got = lax.all_to_all(send, ("sub", "row"), 0, 0, tiled=True)
    sums, out = call(
        finish_kernel, [block, block], got, value, *exchange(packets), taker, used, residual, search, sums
    )
    return (sums[None], out[None])


def solution(mesh):
    in_specs = (
        P("sub", "row", None),
        P("sub", "row", None),
        P("sub", "row", None),
        P("sub", "row", None),
        P("row", None),
        P("sub", "row"),
        P("sub", "row"),
        P("sub", None),
    )
    out_specs = (P("sub", "row", None), P("sub", "row", None))
    return jax.shard_map(local, mesh=mesh, in_specs=in_specs, out_specs=out_specs, check_vma=False)
```

```python
import functools

import jax
import jax.numpy as jnp
from jax import lax
from jax.experimental import pallas as pl
from jax.experimental.pallas import tpu as pltpu
from jax.sharding import PartitionSpec as P

ITERS = 3
LANES = 128
PANEL = 128
GROUP = 4
HIGHEST_PRECISION = lax.Precision.HIGHEST
F32, BF16 = jnp.float32, jnp.bfloat16
VMEM = pl.BlockSpec(memory_space=pltpu.VMEM)
SMEM = pl.BlockSpec(memory_space=pltpu.SMEM)
ANY = pl.BlockSpec(memory_space=pl.ANY)


def call(kernel, outs, *args, scalars=0, scratch=(), flops=10**8, vmem=12, loose=0):
    return pl.pallas_call(
        kernel,
        out_shape=[jax.ShapeDtypeStruct(shape, dtype) for shape, dtype in outs],
        in_specs=[SMEM] * scalars + [VMEM] * (len(args) - scalars - loose) + [ANY] * loose,
        out_specs=[VMEM] * len(outs),
        scratch_shapes=list(scratch),
        cost_estimate=pl.CostEstimate(flops=flops, bytes_accessed=10**6, transcendentals=0),
        compiler_params=pltpu.CompilerParams(vmem_limit_bytes=vmem * 2**20),
    )(*args)


def dot(left, right):
    return jnp.dot(left, right, preferred_element_type=F32)


def exact(left, right):
    return jnp.dot(left, right, precision=HIGHEST_PRECISION, preferred_element_type=F32)


def halves(value):
    high = value.astype(BF16)
    return high, (value - high.astype(F32)).astype(BF16)


def thirds(value):
    high = value.astype(BF16)
    rest = value - high.astype(F32)
    middle = rest.astype(BF16)
    return high, middle, (rest - middle.astype(F32)).astype(BF16)


def select_rows(chooser, value):
    cols = value.shape[1]
    found = dot(chooser, jnp.concatenate(thirds(value), axis=1))
    return found[:, :cols] + (found[:, cols : 2 * cols] + found[:, 2 * cols :])


def write_packets(packets, chooser, value):
    packed = select_rows(chooser, value)
    slots = packed.shape[0] // 4
    for k in range(4):
        packets[k][...] = packed[k * slots : (k + 1) * slots]


def apply_rows(high, low, vector, out):
    first, second = halves(vector)
    both = jnp.concatenate([first, second], axis=1)
    tile = high.shape[0] // 4

    def body(i, carry):
        rows = pl.ds(pl.multiple_of(i * tile, 16), tile)
        wide = dot(high[rows, :], both)
        out[rows, :] = wide[:, :LANES] + (wide[:, LANES:] + dot(low[rows, :], first))
        return carry

    lax.fori_loop(0, 4, body, 0)


def split_and_apply(matrix, vector, high, low, out):
    first, second = halves(vector)
    both = jnp.concatenate([first, second], axis=1)
    tile = matrix.shape[0] // 4

    def body(i, carry):
        rows = pl.ds(pl.multiple_of(i * tile, 16), tile)
        top, bottom = halves(matrix[rows, :])
        high[rows, :] = top
        low[rows, :] = bottom
        wide = dot(top, both)
        out[rows, :] = wide[:, :LANES] + (wide[:, LANES:] + dot(bottom, first))
        return carry

    lax.fori_loop(0, 4, body, 0)


def assemble(row, blocks, full):
    rows = full.shape[0] // 4
    for k in range(4):
        origin = lax.rem(row[0] - k + 4, 4)
        full[pl.ds(pl.multiple_of(origin * rows, 64), rows), :] = blocks[k][:rows, :]


def own_rows(row, full):
    rows = full.shape[0] // 4
    return full[pl.ds(pl.multiple_of(row[0] * rows, 64), rows), :]


def by_row(row, choices):
    picked = choices[0]
    for k in range(1, 4):
        picked = jnp.where(row[0] == k, choices[k], picked)
    return picked


def col_sum(first, second):
    return jnp.sum(first * second, axis=0, keepdims=True)


def prepare_kernel(parity, labels, partner, gap, sender, taker, used, p0, p1, p2, p3):
    n = gap.shape[0]
    slots = n // 4
    down = lax.broadcasted_iota(jnp.int32, (n, n), 0)
    across = lax.broadcasted_iota(jnp.int32, (n, n), 1)
    label, part_r = labels[...], partner[...]
    flipped = jnp.where(label == 0, parity[0], 1 - parity[0])
    role_r = jnp.where(label < 2, flipped, label)
    diagonal = down == across
    role_c = jnp.sum(jnp.where(diagonal, role_r, 0), axis=1, keepdims=True)
    part_c = jnp.sum(jnp.where(diagonal, part_r, 0), axis=1, keepdims=True)
    same = role_c == role_r
    rank = jnp.sum(jnp.where(same & (down < across), 1, 0), axis=0, keepdims=True)
    sender[...] = jnp.where(down == role_r * slots + rank, 1.0, 0.0).astype(BF16)
    rank = jnp.sum(jnp.where(same & (part_r < part_c), 1, 0), axis=1, keepdims=True)
    taker[...] = jnp.where(across == role_c * slots + rank, 1.0, 0.0).astype(BF16)
    used[...] = jnp.broadcast_to(jnp.where(role_c < 4, 1.0, 0.0), used.shape)
    write_packets((p0, p1, p2, p3), sender[...], gap[...])


def jump_of(value, arrived, taker, used):
    got = jnp.concatenate([a[...] for a in arrived], axis=0)
    return jnp.where(used[...] > 0, value[...], 0.0) - select_rows(taker[...], got)


def jump_kernel(value, a0, a1, a2, a3, taker, used, *rest):
    rest[-1][...] = jump_of(value, (a0, a1, a2, a3), taker, used)


def write_pieces(row, out, load, scalars):
    pieces = [
        jnp.concatenate([load[6 * k : 6 * k + 6], scalars[k], jnp.zeros((1, LANES), F32)], axis=0)
        for k in range(4)
    ]
    for k in range(4):
        out[k][...] = by_row(row, pieces[k:] + pieces[:k])


def jump_first_load_kernel(row, value, a0, a1, a2, a3, taker, used, coupling_t, out, *pieces):
    jumped = jump_of(value, (a0, a1, a2, a3), taker, used)
    out[...] = jumped
    write_pieces(row, pieces, exact(coupling_t[...], jumped), [jnp.zeros((1, LANES), F32)] * 4)


def jump_load_kernel(
    row, value, a0, a1, a2, a3, taker, used, coupling_t, residual, pre, image, search, out, *pieces
):
    jumped = jump_of(value, (a0, a1, a2, a3), taker, used)
    out[...] = jumped
    own_residual, own_pre = own_rows(row, residual), own_rows(row, pre)
    own_image, own_search = own_rows(row, image), own_rows(row, search)
    scalars = [
        col_sum(own_residual, own_pre),
        col_sum(own_residual, jumped) + col_sum(own_image, own_pre),
        col_sum(own_image, jumped),
        col_sum(own_search, own_image),
    ]
    write_pieces(row, pieces, exact(coupling_t[...], jumped), scalars)


def dirichlet_first_kernel(
    row, b0, b1, b2, b3, matrix, sender, full, image, high, low, p0, p1, p2, p3
):
    assemble(row, (b0, b1, b2, b3), full)
    split_and_apply(matrix, full[...], high, low, image)
    write_packets((p0, p1, p2, p3), sender[...], image[...])


def dirichlet_kernel(row, b0, b1, b2, b3, high, low, sender, full, image, p0, p1, p2, p3):
    assemble(row, (b0, b1, b2, b3), full)
    apply_rows(high, low, full[...], image)
    write_packets((p0, p1, p2, p3), sender[...], image[...])


def spread_first_kernel(g0, g1, g2, g3, corner_rows, send):
    piece = jnp.concatenate([(g0[...] + g1[...]) + (g2[...] + g3[...]), corner_rows[...]], axis=0)
    for k in range(send.shape[0] // 16):
        send[16 * k : 16 * k + 16, :] = piece


def spread_kernel(g0, g1, g2, g3, send):
    piece = (g0[...] + g1[...]) + (g2[...] + g3[...])
    for k in range(send.shape[0] // 8):
        send[8 * k : 8 * k + 8, :] = piece


def solve_first_kernel(got, inverse, corner_col, mixer, out):
    subs = got.shape[0] // 16
    coarse = inverse.shape[0]
    split = got[...].reshape(subs, 16, LANES)
    loads = split[:, :8].reshape(subs * 8, LANES)
    names = split[:, 8:].reshape(subs * 8, LANES).astype(jnp.int32)
    lane = lax.broadcasted_iota(jnp.int32, (subs * 8, LANES), 1)
    slot = lax.broadcasted_iota(jnp.int32, (subs * 8, LANES), 0)
    real = lax.rem(slot, 8) < 6
    spread = jnp.concatenate(
        [
            jnp.where(real & (names == lane + k * LANES), 1.0, 0.0).astype(BF16)
            for k in range(coarse // LANES)
        ],
        axis=1,
    )
    wide = lax.broadcasted_iota(jnp.int32, (corner_col.shape[0], coarse), 1)
    own = jnp.where(corner_col[...] == wide, 1.0, 0.0).astype(BF16)
    chosen = select_rows(own, inverse[...])
    total = None
    for part in thirds(chosen):
        term = lax.dot_general(
            part, spread, (((1,), (1,)), ((), ())), preferred_element_type=F32
        )
        total = term if total is None else total + term
    mixer[...] = total
    out[:24, :] = exact(total, loads)
    out[24:, :] = jnp.zeros((8, LANES), F32)


def solve_kernel(row, got, mixer, out):
    subs = got.shape[0] // 8
    out[:24, :] = exact(mixer[...], got[...])
    value = jnp.sum(got[...].reshape(subs, 8, LANES), axis=0)[6:7]
    place = lax.broadcasted_iota(jnp.int32, (8, LANES), 0)
    out[24:, :] = jnp.where(place == row[0], jnp.broadcast_to(value, (8, LANES)), 0.0)


def flex_kernel(row, b0, b1, b2, b3, high, low, full, out):
    assemble(row, (b0, b1, b2, b3), full)
    apply_rows(high, low, full[...], out)


def flex_first_kernel(row, b0, b1, b2, b3, matrix, full, out, high, low):
    assemble(row, (b0, b1, b2, b3), full)
    split_and_apply(matrix, full[...], high, low, out)


def join_first_kernel(s0, s1, s2, s3, flexed, coupling, sender, solved, out, p0, p1, p2, p3):
    total = (s0[...] + s1[...]) + (s2[...] + s3[...])
    solved[...] = total[:24]
    out[...] = flexed[...] + exact(coupling[...], solved[...])
    write_packets((p0, p1, p2, p3), sender[...], out[...])


def step_lengths(total):
    rho, cross, square, energy = total[24:25], total[25:26], total[26:27], total[27:28]
    alpha = rho / energy
    next_rho = rho - alpha * cross + alpha * alpha * square
    return alpha, next_rho / rho


def join(s0, s1, s2, s3, flex_pre, flex_search, flex_step, solved_pre, solved, coupling, out):
    total = (s0[...] + s1[...]) + (s2[...] + s3[...])
    alpha, beta = step_lengths(total)
    next_flex_pre = flex_pre[...] - alpha * flex_step[...]
    next_flex = next_flex_pre + beta * flex_search[...]
    next_solved_pre = solved_pre[...] - alpha * total[:24]
    next_solved = next_solved_pre + beta * solved[...]
    out[...] = next_flex + exact(coupling[...], next_solved)
    return alpha, beta, next_flex_pre, next_flex, next_solved_pre, next_solved


def join_kernel(
    s0, s1, s2, s3, flex_pre, flex_search, flex_step, solved_pre, solved, coupling, sender,
    lengths, new_flex_pre, new_flex_search, new_solved_pre, new_solved, out, p0, p1, p2, p3,
):
    alpha, beta, *new = join(s0, s1, s2, s3, flex_pre, flex_search, flex_step, solved_pre, solved, coupling, out)
    write_packets((p0, p1, p2, p3), sender[...], out[...])
    new_flex_pre[...], new_flex_search[...], new_solved_pre[...], new_solved[...] = new
    lengths[...] = jnp.concatenate([alpha] * 4 + [beta] * 4, axis=0)


def update_kernel(row, lengths, step, residual, pre, image, search, new_residual, new_pre, new_search, sums):
    alpha, beta = lengths[0:1, :], lengths[4:5, :]
    sums[...] = alpha * own_rows(row, search)
    new_residual[...] = residual[...] - alpha * image[...]
    new_pre[...] = pre[...] - alpha * step[...]
    new_search[...] = new_pre[...] + beta * search[...]


def join_last_kernel(
    row, s0, s1, s2, s3, flex_pre, flex_search, flex_step, solved_pre, solved, coupling, sender,
    step, residual, pre, image, search, sums,
    bundle, p0, p1, p2, p3, send,
):
    n = sums.shape[0]
    new_residual, new_search, new_sums, out = (bundle.at[k * n : (k + 1) * n] for k in range(4))
    alpha, beta, *_ = join(s0, s1, s2, s3, flex_pre, flex_search, flex_step, solved_pre, solved, coupling, out)
    write_packets((p0, p1, p2, p3), sender[...], out[...])
    own_search = own_rows(row, search)
    new_sums[...] = sums[...] + alpha * own_search
    own_pre = own_rows(row, pre) - alpha * step[...]
    new_residual[...] = own_rows(row, residual) - alpha * own_rows(row, image)
    new_search[...] = own_pre + beta * own_search
    pair = jnp.concatenate(
        [col_sum(new_residual[...], own_pre), 2.0 * col_sum(new_search[...], out[...])] * 4, axis=0
    )
    for k in range(send.shape[0] // 8):
        send[8 * k : 8 * k + 8, :] = pair


def finish_kernel(got, bundle, a0, a1, a2, a3, taker, used, out_sums, out_residual):
    total = jnp.sum(got[...].reshape(got.shape[0] // 8, 8, LANES), axis=0)
    total = (total[0:2] + total[2:4]) + (total[4:6] + total[6:8])
    alpha = total[0:1] / total[1:2]
    n = used.shape[0]
    residual, search, sums, value = (bundle.at[k * n : (k + 1) * n] for k in range(4))
    image = jump_of(value, (a0, a1, a2, a3), taker, used)
    out_sums[...] = sums[...] + alpha * search[...]
    out_residual[...] = residual[...] - alpha * image


def invert_panel(matrix):
    size = matrix.shape[0]
    across = lax.broadcasted_iota(jnp.int32, (size, size), 1)
    lane, across8 = across[:1], across[:8]
    down8 = lax.broadcasted_iota(jnp.int32, (8, size), 0)
    for start in range(0, size, GROUP):
        base = start // 8 * 8
        columns = [
            jnp.broadcast_to(matrix[:, start + j : start + j + 1], (size, size)) for j in range(GROUP)
        ]
        pivots = matrix[base : base + 8, :]
        rest = jnp.where((across >= start) & (across < start + GROUP), 0.0, matrix)
        for j in range(GROUP):
            k = start + j
            column = columns[j]
            inverse = 1.0 / column[k : k + 1, :]
            scaled = jnp.where(lane == k, 1.0, pivots[k - base : k - base + 1, :]) * inverse
            cleared = jnp.where(across8 == k, 0.0, pivots) - column[base : base + 8, :] * scaled
            pivots = jnp.where(down8 == k - base, scaled, cleared)
            rest = rest - column * jnp.where((lane > k) & (lane < start + GROUP), 0.0, scaled)
            for m in range(j + 1, GROUP):
                factor = columns[m][k : k + 1, :] * inverse
                updated = columns[m] - column * factor
                parts = [updated[:base]] if base else []
                parts.append(jnp.where(down8 == k - base, factor, updated[base : base + 8]))
                if base + 8 < size:
                    parts.append(updated[base + 8 :])
                columns[m] = jnp.concatenate(parts, axis=0)
        parts = [rest[:base]] if base else []
        parts.append(pivots)
        if base + 8 < size:
            parts.append(rest[base + 8 :])
        matrix = jnp.concatenate(parts, axis=0)
    return matrix


def eliminate(number, source, out):
    size = source.shape[0]
    panel = slice(number * PANEL, (number + 1) * PANEL)
    column = source[:, panel]
    inverse = invert_panel(source[panel, panel])
    scaled = exact(inverse, source[panel, :])
    here = lax.broadcasted_iota(jnp.int32, (PANEL, size), 1) // PANEL == number
    scaled = jnp.where(here, jnp.concatenate([inverse] * (size // PANEL), axis=1), scaled)
    for i in range(size // PANEL):
        rows = slice(i * PANEL, (i + 1) * PANEL)
        if i == number:
            out[rows, :] = scaled
        else:
            out[rows, :] = jnp.where(here, 0.0, source[rows, :]) - exact(column[rows, :], scaled)


def invert_first_kernel(row, b0, b1, b2, b3, out, whole):
    assemble(row, (b0, b1, b2, b3), whole)
    eliminate(0, whole, out)


def invert_kernel(number, source, out):
    eliminate(number, source, out)


def row_pieces(pieces):
    count = lax.axis_size("row")
    moved = [pieces[0]]
    for k in range(1, 4):
        moved.append(lax.ppermute(pieces[k], "row", [(i, (i + k) % count) for i in range(count)]))
    return moved


def row_blocks(value):
    count = lax.axis_size("row")
    moved = [value]
    for k in range(1, 4):
        moved.append(lax.ppermute(value, "row", [(i, (i + k) % count) for i in range(count)]))
    return moved


def exchange(packets):
    count = lax.axis_size("sub")
    mate = [(i, i ^ 1) for i in range(count)]
    other = [(i, (i + (1 if i % 2 else -1)) % count) for i in range(count)]
    ahead = [(i, (i + 2) % count) for i in range(count)]
    behind = [(i, (i - 2) % count) for i in range(count)]
    return (
        lax.ppermute(packets[0], "sub", mate),
        lax.ppermute(packets[1], "sub", other),
        lax.ppermute(packets[3], "sub", behind),
        lax.ppermute(packets[2], "sub", ahead),
    )


def local(displacement_gap, flexibility, dirichlet, coupling, coarse_matrix, labels, partner, corners):
    gap = displacement_gap[0]
    n = gap.shape[0]
    order = flexibility.shape[2]
    subs = lax.axis_size("sub")
    coarse = coarse_matrix.shape[1]
    row_index = lax.axis_index("row").astype(jnp.int32)
    row = row_index.reshape(1)
    block, full, packet = ((n, LANES), F32), ((order, LANES), F32), ((n // 4, LANES), F32)
    square = ((n, n), BF16)

    coarse_blocks = row_blocks(coarse_matrix)

    parity = lax.axis_index("sub").astype(jnp.int32) % 2
    sender, taker, used, *packets = call(
        prepare_kernel, [square, square, block] + [packet] * 4,
        parity.reshape(1), labels, partner, gap, scalars=1, flops=10**9, vmem=20,
    )

    part = ((n, order), BF16)
    couple = coupling[0]
    couple_t = couple.T

    def jump(value, packets, *after):
        return call(
            jump_kernel, [block], value, *exchange(packets), taker, used, *after, loose=len(after)
        )[0]

    piece = ((8, LANES), F32)

    def apply_dirichlet(own):
        whole, image, *packets = call(
            dirichlet_kernel, [full, block] + [packet] * 4,
            row, *row_blocks(own), *dirichlet_parts, sender, scalars=1, flops=2 * 10**9, vmem=20,
        )
        return whole, image, packets

    own_residual = jump(gap, packets, *coarse_blocks)
    residual, image, *rest = call(
        dirichlet_first_kernel, [full, block] + [part] * 2 + [packet] * 4,
        row, *row_blocks(own_residual), dirichlet[0], sender, scalars=1, flops=3 * 10**9, vmem=28,
    )
    dirichlet_parts, packets = rest[:2], rest[2:]

    [inverse] = call(
        invert_first_kernel, [((coarse, coarse), F32)], row, *coarse_blocks,
        scalars=1, flops=6 * 10**9, vmem=18, scratch=[pltpu.VMEM((coarse, coarse), F32)],
    )
    for number in range(1, coarse // PANEL):
        [inverse] = call(
            functools.partial(invert_kernel, number), [((coarse, coarse), F32)], inverse, flops=6 * 10**9, vmem=18,
        )

    own_corners = corners[0]
    mine = lax.dynamic_slice(own_corners, (6 * row_index,), (6,)).astype(F32)
    corner_rows = jnp.broadcast_to(jnp.concatenate([mine, mine[:2]])[:, None], (8, LANES))

    own_pre, *parts = call(
        jump_first_load_kernel, [block] + [piece] * 4,
        row, image, *exchange(packets), taker, used, couple_t, scalars=1,
    )
    [send] = call(spread_first_kernel, [((16 * subs, LANES), F32)], *row_pieces(parts), corner_rows)
    got = lax.all_to_all(send, "sub", 0, 0, tiled=True)
    mixer, solved = call(
        solve_first_kernel, [((24, 8 * subs), F32), ((32, LANES), F32)], got, inverse, own_corners[:, None], vmem=16
    )
    small = ((24, LANES), F32)

    def apply_flex(own):
        return call(
            flex_kernel, [full, block], row, *row_blocks(own), *flex_parts, scalars=1, flops=2 * 10**9, vmem=20
        )

    pre, flex_pre, *flex_parts = call(
        flex_first_kernel, [full, block] + [part] * 2,
        row, *row_blocks(own_pre), flexibility[0], scalars=1, flops=3 * 10**9, vmem=28,
    )
    solved_pre, value, *packets = call(
        join_first_kernel, [small, block] + [packet] * 4, *row_blocks(solved), flex_pre, couple, sender
    )
    search, flex_search, solved_search = pre, flex_pre, solved_pre
    for sweep in range(1, ITERS):
        image, value, packets = apply_dirichlet(jump(value, packets))
        own_step, *parts = call(
            jump_load_kernel, [block] + [piece] * 4,
            row, value, *exchange(packets), taker, used, couple_t, residual, pre, image, search, scalars=1, vmem=16,
        )
        [send] = call(spread_kernel, [((8 * subs, LANES), F32)], *row_pieces(parts))
        got = lax.all_to_all(send, "sub", 0, 0, tiled=True)
        step, flex_step = apply_flex(own_step)
        [solved] = call(solve_kernel, [((32, LANES), F32)], row, got, mixer, scalars=1)
        joined = (*row_blocks(solved), flex_pre, flex_search, flex_step, solved_pre, solved_search, couple, sender)
        if sweep < ITERS - 1:
            lengths, flex_pre, flex_search, solved_pre, solved_search, value, *packets = call(
                join_kernel, [((8, LANES), F32)] + [block] * 2 + [small] * 2 + [block] + [packet] * 4, *joined
            )
            residual, pre, search, sums = call(
                update_kernel, [full] * 3 + [block], row, lengths, step, residual, pre, image, search,
                scalars=1, vmem=16,
            )
        else:
            bundle, *packets, send = call(
                join_last_kernel, [((4 * n, LANES), F32)] + [packet] * 4 + [((8 * subs, LANES), F32)],
                row, *joined, own_step, residual, pre, image, search, sums, scalars=1, vmem=16,
            )
    got = lax.all_to_all(send, ("sub", "row"), 0, 0, tiled=True)
    sums, out = call(
        finish_kernel, [block, block], got, bundle, *exchange(packets), taker, used
    )
    return (sums[None], out[None])


def solution(mesh):
    in_specs = (
        P("sub", "row", None),
        P("sub", "row", None),
        P("sub", "row", None),
        P("sub", "row", None),
        P("row", None),
        P("sub", "row"),
        P("sub", "row"),
        P("sub", None),
    )
    out_specs = (P("sub", "row", None), P("sub", "row", None))
    return jax.shard_map(local, mesh=mesh, in_specs=in_specs, out_specs=out_specs, check_vma=False)
```
